32 devices in a mesh: gx: 4 (over z), gy: 4 (over y, x), gz: 2 (over core).
Axes of the slice: x: 2, y: 2, z: 4, core: 2. Of those that a mesh axis runs over, the one named last changes fastest.
Arguments:
- volt: float32 [32, 128, 512], P('gz', 'gx', 'gy'), may hold values from 0 to 1
- recovery: float32 [32, 128, 512], P('gz', 'gx', 'gy'), may hold values from 0 to 1
- fiber_class: int32 [32, 128, 512], P('gz', 'gx', 'gy'), may hold values from 0 to 7
- fiber_table: float32 [3, 8], replicated, may hold values from 0.02 to 0.16
- junction_block: int32 [4096], P(('gx', 'gy', 'gz')), may hold values from 0 to 511
- junction_term: int32 [4096], P(('gx', 'gy', 'gz')), may hold values from 0 to 31
- junction_owner: int32 [4096, 1], P(('gx', 'gy', 'gz')), may hold values from 0 to 15; in each aligned block of 128 rows (0 to 127, 128 to 255, ...) at most 16 rows name the same one
- term_volt: float32 [1024, 128], P(('gx', 'gy', 'gz')), may hold values from 0 to 1
- term_recovery: float32 [1024, 128], P(('gx', 'gy', 'gz')), may hold values from 0 to 1
- term_gain: float32 [1024], P(('gx', 'gy', 'gz')), may hold values from 0.5 to 4
- cable_gain: float32 [1024], P(('gx', 'gy', 'gz')), may hold values from 0.05 to 0.45
Outputs:
- volt_out: float32 [32, 128, 512], P('gz', 'gx', 'gy')
- recovery_out: float32 [32, 128, 512], P('gz', 'gx', 'gy')
- term_volt_out: float32 [1024, 128], P(('gx', 'gy', 'gz'))
- term_recovery_out: float32 [1024, 128], P(('gx', 'gy', 'gz'))
The draws below stay inside these ranges and needn't reach their ends.
Inputs may be any that keep to these rules, and one draw needn't show every extreme that they name: `junction_owner`: among the 128 junctions of one device, at most 16 have the same owner, a bound that some block reaches.
All inputs are finite; a program needn't handle non-finite values.
Results may differ from the reference program's by a relative error of at most 0.00002.
Values sent between devices are 32-bit elements; how exact they have to be, the bound alone decides.
A program may use at most 64 MiB of HBM per device.

```python
import math
import jax
import jax.numpy as jnp
import numpy as np

CX = 32
CY = 128
CZ = 16
NCLASS = 8
TERM_DEV = 32
JD = 128
STEPS = 4
CAP = 16
NX = 128
NY = 512
NZ = 32
JUNCTIONS = 4096
TERMINALS = 1024
N_GX = 4
N_GY = 4
N_GZ = 2


def with_ends(array, key, smallest, largest):
    index_at = [jax.random.randint(jax.random.fold_in(key, axis), (), 0, length) for axis, length in enumerate(array.shape)]
    widest = array.shape.index(max(array.shape))
    neighbour = index_at[:widest] + [(index_at[widest] + 1) % array.shape[widest]] + index_at[widest + 1:]
    return array.at[tuple(index_at)].set(smallest).at[tuple(neighbour)].set(largest)


def block_levels(rng, dims, pieces, smallest, largest):
    def one(position, shards_of):
        draws = jax.random.uniform(jax.random.fold_in(jax.random.fold_in(rng, 6), position), (shards_of,), jnp.float32, smallest / len(pieces), largest / len(pieces))
        return jnp.repeat(jnp.exp(draws), dims[position] // shards_of).reshape((-1,) + (1,) * (len(dims) - position - 1))

    loudness = one(*pieces[0])
    for cut in pieces[1:]:
        loudness = loudness * one(*cut)
    return loudness


def assign_block(own_key, own, number, rows, amount, top, most, skew):
    sequence = jax.random.permutation(own_key, amount)
    heavy_load, common = shares(amount, rows * top, most, skew, True), shares(amount, rows * top, most, skew, False)
    places = jnp.arange(amount)

    def named(sizes, rotation):
        used = int((sizes > 0).sum())
        fixed = max(1, used // 4)
        moved = fixed + (places - fixed + rotation * (used - fixed)) % max(1, amount - fixed)
        return jnp.zeros((amount,), jnp.int32).at[sequence[jnp.where(places < fixed, places, moved)]].set(jnp.asarray(sizes, jnp.int32))

    sizes = jnp.where(number % 4 == 0, named(heavy_load, number // 4), named(common, number - number // 4 - 1))
    mixed = jax.random.permutation(jax.random.fold_in(own, 3), amount)
    donor, sink = mixed[0:amount // 2 * 2:2], mixed[1:amount // 2 * 2:2]
    margin = jnp.minimum(sizes[donor] - 1, most - sizes[sink]) // 2
    margin = jnp.where((donor == sequence[0]) | (sink == sequence[0]) | (sizes[sink] == 0), 0, jnp.maximum(margin, 0))
    moved = jax.random.randint(jax.random.fold_in(own, 4), (amount // 2,), 0, 1 << 20) % (margin + 1)
    sizes = sizes.at[donor].add(-moved).at[sink].add(moved)
    members = jnp.searchsorted(jnp.cumsum(sizes), jnp.arange(rows * top), side="right").astype(jnp.int32)
    table = members.reshape(top, rows).T
    table = table[jax.random.permutation(jax.random.fold_in(own, 1), rows)]
    rotation = jax.random.randint(jax.random.fold_in(own, 2), (rows, 1), 0, top)
    return jnp.take_along_axis(table, (jnp.arange(top)[None, :] + rotation) % top, axis=1)


def shares(count, total, reach, skew, full):
    loads = [(1 << 20) // math.isqrt(rank ** skew) + 1 for rank in range(1, count + 1)]
    largest = reach if full else min(reach, max(-(-total // count), total * loads[0] // sum(loads)))
    least = 1 if total - largest >= count - 1 else 0
    counts, rest = [largest] + [least] * (count - 1), total - largest - least * (count - 1)
    while rest > 0:
        candidates = [i for i in range(1, count) if counts[i] < largest] or [i for i in range(1, count) if counts[i] < reach]
        pool, budget = sum([loads[i] for i in candidates]), rest
        for i in candidates:
            more = min(reach - counts[i], max(1, budget * loads[i] // pool), rest)
            counts[i] = counts[i] + more
            rest = rest - more
    return np.array(counts)


def setup_inputs(seed: int = 0) -> dict:
    splits = jax.random.split(jax.random.key(seed), 12)
    volt = jnp.clip(1.0 * jax.random.uniform(splits[0], (NZ, NX, NY), jnp.float32) ** block_levels(splits[0], (NZ, NX, NY), ((0, 2), (1, 4), (2, 4)), -0.2, 0.2), 0.0, 1.0)
    recovery = jnp.clip(1.0 * jax.random.uniform(splits[1], (NZ, NX, NY), jnp.float32) ** block_levels(splits[1], (NZ, NX, NY), ((0, 2), (1, 4), (2, 4)), -0.2, 0.2), 0.0, 1.0)
    fiber_class = with_ends(jax.random.randint(splits[2], (NZ, NX, NY), 0, NCLASS), jax.random.fold_in(splits[2], 1), 0, NCLASS - 1).astype(jnp.int32)
    fiber_table = jnp.clip(jax.random.uniform(splits[3], (3, NCLASS), jnp.float32, 0.02, 0.16), 0.02, 0.16)
    junction_block = with_ends(jax.random.randint(splits[4], (JUNCTIONS,), 0, CZ * CX), jax.random.fold_in(splits[4], 1), 0, (CZ * CX) - 1).astype(jnp.int32)
    junction_term = with_ends(jax.random.randint(splits[5], (JUNCTIONS,), 0, TERM_DEV), jax.random.fold_in(splits[5], 1), 0, TERM_DEV - 1).astype(jnp.int32)
    junction_owner_keys = jax.random.split(jax.random.fold_in(splits[6], 1), JUNCTIONS // JD)
    junction_owner_turns = jax.random.permutation(jax.random.fold_in(splits[6], 3), JUNCTIONS // JD)
    junction_owner = jax.vmap(lambda own, number: assign_block(jax.random.fold_in(splits[6], 2), own, number, JD, N_GX * N_GY, 1, CAP, 2))(junction_owner_keys, junction_owner_turns).reshape((JUNCTIONS, 1))
    term_volt = jnp.clip(1.0 * jax.random.uniform(splits[7], (TERMINALS, CY), jnp.float32) ** block_levels(splits[7], (TERMINALS, CY), ((0, 32),), -0.2, 0.2), 0.0, 1.0)
    term_recovery = jnp.clip(1.0 * jax.random.uniform(splits[8], (TERMINALS, CY), jnp.float32) ** block_levels(splits[8], (TERMINALS, CY), ((0, 32),), -0.2, 0.2), 0.0, 1.0)
    term_gain = jnp.clip(jnp.exp(math.log(4.0) - 2.0794415 * jax.random.uniform(splits[9], (TERMINALS,), jnp.float32) ** block_levels(splits[9], (TERMINALS,), ((0, 32),), -0.2, 0.2)), 0.5, 4.0)
    cable_gain = jnp.clip(jnp.exp(math.log(0.45) - 2.1972245 * jax.random.uniform(splits[10], (TERMINALS,), jnp.float32) ** block_levels(splits[10], (TERMINALS,), ((0, 32),), -0.2, 0.2)), 0.05, 0.45)
    return dict(volt=volt, recovery=recovery, fiber_class=fiber_class, fiber_table=fiber_table, junction_block=junction_block, junction_term=junction_term, junction_owner=junction_owner, term_volt=term_volt, term_recovery=term_recovery, term_gain=term_gain, cable_gain=cable_gain)


def cell_kinetics(v, w, drive):
    react = -8.0 * v * (v - 0.15) * (v - 1.0) - v * w
    new_v = 0.1 * (react + drive)
    new_w = w + 0.01 * (-w - 8.0 * v * (v - 1.15))
    return new_v, new_w


def reference(volt, recovery, fiber_class, fiber_table, junction_block, junction_term, junction_owner, term_volt, term_recovery, term_gain, cable_gain):
    coef_z = jnp.zeros(volt.shape, jnp.float32)
    coef_x = jnp.zeros(volt.shape, jnp.float32)
    coef_y = jnp.zeros(volt.shape, jnp.float32)
    for klass in range(NCLASS):
        hit = fiber_class == klass
        coef_z = jnp.where(hit, fiber_table[0, klass], coef_z)
        coef_x = jnp.where(hit, fiber_table[1, klass], coef_x)
        coef_y = jnp.where(hit, fiber_table[2, klass], coef_y)
    index = jnp.arange(JUNCTIONS, dtype=jnp.int32)
    block_dev = index // JD
    tile_x = block_dev // (N_GY * N_GZ)
    tile_y = (block_dev // N_GZ) % N_GY
    tile_z = block_dev % N_GZ
    depth_at = tile_z * CZ + junction_block // CX
    row_at = tile_x * CX + junction_block % CX
    target = (junction_owner[:, 0] * N_GZ + tile_z) * TERM_DEV + junction_term
    gains = term_gain[target]
    for step in range(STEPS):
        grid = volt.reshape(NZ, NX, N_GY, CY)
        rows = grid[depth_at, row_at, tile_y]
        current = gains[:, None] * (term_volt[target] - rows)
        into_voxel = jnp.zeros((NZ, NX, N_GY, CY), jnp.float32).at[depth_at, row_at, tile_y].add(current).reshape(NZ, NX, NY)
        into_term = jnp.zeros((TERMINALS, CY), jnp.float32).at[target].add(-current)
        padded = jnp.pad(volt, 1, mode="edge")
        lap_z = (padded[2:, 1:-1, 1:-1] + padded[:-2, 1:-1, 1:-1]) - 2.0 * volt
        lap_x = (padded[1:-1, 2:, 1:-1] + padded[1:-1, :-2, 1:-1]) - 2.0 * volt
        lap_y = (padded[1:-1, 1:-1, 2:] + padded[1:-1, 1:-1, :-2]) - 2.0 * volt
        react_v, new_w = cell_kinetics(volt, recovery, into_voxel)
        new_v = volt + (coef_z * lap_z + coef_x * lap_x + coef_y * lap_y) + react_v
        cable = jnp.pad(term_volt, ((0, 0), (1, 1)), mode="edge")
        lap_k = (cable[:, 2:] + cable[:, :-2]) - 2.0 * term_volt
        react_u, new_r = cell_kinetics(term_volt, term_recovery, 0.1 * into_term)
        new_u = term_volt + cable_gain[:, None] * lap_k + react_u
        volt, recovery, term_volt, term_recovery = new_v, new_w, new_u, new_r
    return volt, recovery, term_volt, term_recovery
```

```python
import functools
import jax
import jax.numpy as jnp
from jax import lax
from jax.experimental import pallas as pl
from jax.experimental.pallas import tpu as pltpu
from jax.sharding import PartitionSpec as P

STEPS = 4
MESH = pl.DeviceIdType.MESH
F32 = jnp.float32
BF16 = jnp.bfloat16
EXACT = lax.Precision.HIGHEST
GAIN_LANE = 64


def iota(shape, dim):
    return lax.broadcasted_iota(jnp.int32, shape, dim)


def one_hot(cond):
    return jnp.where(cond, 1.0, 0.0).astype(BF16)


def dot_nt(a, b):
    return lax.dot_general(a, b, (((1,), (1,)), ((), ())), preferred_element_type=F32)


def select_dot(mask, values):
    high = values.astype(BF16)
    rest = values - high.astype(F32)
    mid = rest.astype(BF16)
    low = (rest - mid.astype(F32)).astype(BF16)
    return (
        jnp.dot(mask, low, preferred_element_type=F32)
        + jnp.dot(mask, mid, preferred_element_type=F32)
    ) + jnp.dot(mask, high, preferred_element_type=F32)


def kernel(
    n_gx,
    n_gy,
    n_gz,
    cap,
    table,
    volt_in,
    rec_in,
    fiber,
    block_row,
    term_row,
    owner_row,
    tv_in,
    tr_in,
    gain_row,
    cable_row,
    volt_out,
    rec_out,
    tv_out,
    tr_out,
    vp,
    coef,
    into,
    a_mat,
    at_mat,
    tg_mat,
    tgt_mat,
    gain_h,
    gain_o,
    msg_send,
    msg_recv,
    v_send,
    v_recv,
    u_send,
    u_recv,
    hx_send,
    hx_recv,
    hy_send,
    hy_recv,
    msg_sem,
    v_sem_s,
    v_sem_r,
    u_sem_s,
    u_sem_r,
    halo_s,
    halo_r,
):
    gx = lax.axis_index("gx")
    gy = lax.axis_index("gy")
    gz = lax.axis_index("gz")
    n = n_gx * n_gy
    me = gx * n_gy + gy
    depth, rows, width = volt_in.shape
    voxel_rows = depth * rows
    groups = voxel_rows // 8
    per = rows // 8
    slots = n * cap
    terms = tv_in.shape[0]
    jcount = block_row.shape[1]
    shift = cap.bit_length() - 1

    def at_peer(d):
        p = lax.rem(me + d, n)
        return p, {"gx": p // n_gy, "gy": lax.rem(p, n_gy)}

    barrier = pltpu.get_barrier_semaphore()

    def greet(d, carry):
        _, where_to = at_peer(d)
        pl.semaphore_signal(barrier, inc=1, device_id=where_to, device_id_type=MESH)
        return carry

    lax.fori_loop(1, n, greet, 0)

    pl.semaphore_signal(barrier, inc=1, device_id={"gz": n_gz - 1 - gz}, device_id_type=MESH)

    def rows_of(p):
        return pl.ds(pl.multiple_of(p * cap, 8), cap)

    def slot_copy(src, dst, s, d, send_sem, recv_sem):
        p, where_to = at_peer(d)
        return pltpu.make_async_remote_copy(
            src_ref=src.at[s, rows_of(p)],
            dst_ref=dst.at[s, rows_of(me)],
            send_sem=send_sem.at[s],
            recv_sem=recv_sem.at[s],
            device_id=where_to,
            device_id_type=MESH,
        )

    def send_slots(src, dst, s, send_sem, recv_sem):
        def go(d, carry):
            slot_copy(src, dst, s, d, send_sem, recv_sem).start()
            return carry

        lax.fori_loop(1, n, go, 0)
        dst[s, rows_of(me)] = src[s, rows_of(me)]

    def all_slots(src, dst, s, send_sem, recv_sem):
        part = pl.ds(0, (n - 1) * cap)
        _, where_to = at_peer(1)
        return pltpu.make_async_remote_copy(
            src_ref=src.at[s, part],
            dst_ref=dst.at[s, part],
            send_sem=send_sem.at[s],
            recv_sem=recv_sem.at[s],
            device_id=where_to,
            device_id_type=MESH,
        )

    def halo_copies(s):
        def make(src, dst, k, where_to):
            return pltpu.make_async_remote_copy(
                src_ref=src,
                dst_ref=dst,
                send_sem=halo_s.at[s, k],
                recv_sem=halo_r.at[s, k],
                device_id=where_to,
                device_id_type=MESH,
            )

        last = depth + 1
        return (
            (make(vp.at[s, depth], vp.at[s, 0], 0, {"gz": n_gz - 1 - gz}), gz == 0, gz == n_gz - 1),
            (make(vp.at[s, 1], vp.at[s, last], 1, {"gz": n_gz - 1 - gz}), gz == n_gz - 1, gz == 0),
            (make(hx_send.at[s, 1], hx_recv.at[s, 0], 2, {"gx": lax.rem(gx + 1, n_gx)}), gx < n_gx - 1, gx > 0),
            (make(hx_send.at[s, 0], hx_recv.at[s, 1], 3, {"gx": lax.rem(gx + n_gx - 1, n_gx)}), gx > 0, gx < n_gx - 1),
            (make(hy_send.at[s], hy_recv.at[s, 0], 4, {"gy": lax.rem(gy + 1, n_gy)}), gy < n_gy - 1, gy > 0),
            (make(hy_send.at[s], hy_recv.at[s, 1], 5, {"gy": lax.rem(gy + n_gy - 1, n_gy)}), gy > 0, gy < n_gy - 1),
        )

    lane8 = iota((8, width), 1)

    def pack(plane, z, packed):
        for i in range(per):
            k = z * per + i
            piece = plane[i * 8 : i * 8 + 8]
            packed = jnp.where(lane8 == k, piece[:, 0:1], packed)
            packed = jnp.where(lane8 == k + groups, piece[:, width - 1 : width], packed)
        return packed

    def send_halos(s):
        for copy, sends, _ in halo_copies(s):
            pl.when(sends)(copy.start)

        @pl.when(gz == 0)
        def _():
            vp[s, 0] = vp[s, 1]

        @pl.when(gz == n_gz - 1)
        def _():
            vp[s, depth + 1] = vp[s, depth]

    packed = jnp.zeros((8, width), F32)
    for z in range(depth):
        plane = volt_in[z]
        vp[0, z + 1] = plane
        hx_send[0, 0, z : z + 1, :] = plane[0:1]
        hx_send[0, 1, z : z + 1, :] = plane[rows - 1 : rows]
        packed = pack(plane, z, packed)
    hy_send[0] = packed
    rec_out[...] = rec_in[...]
    tv_out[...] = tv_in[...]
    tr_out[...] = tr_in[...]

    owner = jnp.broadcast_to(owner_row[...], (jcount, jcount))
    owner_t = jnp.transpose(owner)
    earlier = (owner_t == owner) & (iota((jcount, jcount), 0) < iota((jcount, jcount), 1))
    rank = jnp.sum(jnp.where(earlier, 1.0, 0.0), axis=0, keepdims=True).astype(jnp.int32)
    slot = owner_row[...] * cap + rank
    holds = iota((slots, jcount), 0) == slot
    holds_b = one_hot(holds)
    tie = one_hot(iota((voxel_rows, jcount), 0) == block_row[...])
    a_mat[...] = dot_nt(holds_b, tie).astype(BF16)
    at_mat[...] = dot_nt(tie, holds_b).astype(BF16)
    term_f = term_row[...].astype(F32) + 1.0
    own_id = jnp.sum(jnp.where(holds, term_f, 0.0), axis=1, keepdims=True)
    slot_lane = iota((slots, 128), 1)
    place = iota((slots, 128), 0) & (cap - 1)
    by_place = jnp.where(slot_lane == place, own_id, 0.0).astype(BF16)
    peer_t = one_hot((iota((n, slots), 1) >> shift) == iota((n, slots), 0))
    ids_out = jnp.dot(peer_t, by_place, preferred_element_type=F32)
    spread = jnp.where(iota((terms, 128), 1) == iota((terms, 128), 0) + GAIN_LANE, 1.0, 0.0)
    gains_lane = jnp.dot(
        jnp.broadcast_to(gain_row[...], (8, terms)), spread, precision=EXACT, preferred_element_type=F32
    )[0:1]
    msg = ids_out + gains_lane
    for p in range(n):
        msg_send[p] = msg[p : p + 1]

    v_send[0] = select_dot(a_mat[...], vp[0, 1 : depth + 1].reshape(voxel_rows, width))

    pl.semaphore_wait(barrier, n)

    def msg_copy(d):
        p, where_to = at_peer(d)
        return pltpu.make_async_remote_copy(
            src_ref=msg_send.at[p],
            dst_ref=msg_recv.at[me],
            send_sem=msg_sem.at[0],
            recv_sem=msg_sem.at[1],
            device_id=where_to,
            device_id_type=MESH,
        )

    def send_msg(d, carry):
        msg_copy(d).start()
        return carry

    lax.fori_loop(1, n, send_msg, 0)
    msg_recv[me] = msg_send[me]
    send_halos(0)
    send_slots(v_send, v_recv, 0, v_sem_s, v_sem_r)

    for z in range(depth):
        klass = fiber[z]
        for k in range(3):
            value = jnp.full(klass.shape, table[k, 0], F32)
            for c in range(1, table.shape[1]):
                value = jnp.where(klass == c, table[k, c], value)
            coef[k, z] = value

    cable = jnp.sum(
        jnp.where(iota((terms, terms), 0) == iota((terms, terms), 1), cable_row[...], 0.0),
        axis=1,
        keepdims=True,
    )

    def all_msgs():
        _, where_to = at_peer(1)
        part = pl.ds(0, n - 1)
        return pltpu.make_async_remote_copy(
            src_ref=msg_send.at[part],
            dst_ref=msg_recv.at[part],
            send_sem=msg_sem.at[0],
            recv_sem=msg_sem.at[1],
            device_id=where_to,
            device_id_type=MESH,
        )

    all_msgs().wait_recv()
    arrived = msg_recv[...].reshape(n, 128)
    peer = jnp.where((iota((slots, n), 0) >> shift) == iota((slots, n), 1), 1.0, 0.0)
    per_slot = jnp.dot(peer, arrived, precision=EXACT, preferred_element_type=F32)
    far_id = jnp.sum(jnp.where(slot_lane == place, per_slot, 0.0), axis=1, keepdims=True)
    far_id = (far_id + 0.5).astype(jnp.int32) - 1
    own_at = (own_id + 0.5).astype(jnp.int32) - 1
    gain_own = jnp.sum(
        jnp.where((slot_lane == own_at + GAIN_LANE) & (own_at >= 0), per_slot, 0.0), axis=1, keepdims=True
    )
    gain_far = jnp.sum(
        jnp.where((slot_lane == far_id + GAIN_LANE) & (far_id >= 0), gains_lane, 0.0), axis=1, keepdims=True
    )
    gain_h[...] = jnp.broadcast_to(gain_own, (slots, width))
    gain_o[...] = jnp.broadcast_to(gain_far, (slots, width))
    tg = one_hot(iota((slots, terms), 1) == far_id)
    tg_mat[...] = tg
    tgt_mat[...] = dot_nt(one_hot(iota((terms, terms), 0) == iota((terms, terms), 1)), tg).astype(BF16)

    u_send[0] = select_dot(tg, tv_out[...])
    send_slots(u_send, u_recv, 0, u_sem_s, u_sem_r)

    row_id = iota((rows, width), 0)
    lane_id = iota((rows, width), 1)

    def step(s, carry):
        for copy, _, receives in halo_copies(s):
            pl.when(receives)(copy.wait_recv)
        all_slots(u_send, u_recv, s, u_sem_s, u_sem_r).wait_recv()
        into[...] = select_dot(at_mat[...], gain_h[...] * (u_recv[s] - v_send[s]))
        mirrored = pltpu.roll(hy_send[s], groups, 1)
        left = jnp.where(gy == 0, mirrored, hy_recv[s, 0])
        right = jnp.where(gy == n_gy - 1, mirrored, hy_recv[s, 1])
        packed = jnp.zeros((8, width), F32)
        for z in range(depth):
            v = vp[s, z + 1]
            w = rec_out[z]
            lap_z = (vp[s, z + 2] + vp[s, z]) - 2.0 * v
            above = jnp.where(gx == n_gx - 1, v[rows - 1 : rows], hx_recv[s, 1, z : z + 1, :])
            below = jnp.where(gx == 0, v[0:1], hx_recv[s, 0, z : z + 1, :])
            up = jnp.where(row_id == rows - 1, above, pltpu.roll(v, rows - 1, 0))
            down = jnp.where(row_id == 0, below, pltpu.roll(v, 1, 0))
            lap_x = (up + down) - 2.0 * v
            k = z * per
            low = jnp.concatenate([left[:, groups + k + i : groups + k + i + 1] for i in range(per)], axis=0)
            high = jnp.concatenate([right[:, k + i : k + i + 1] for i in range(per)], axis=0)
            before = jnp.where(lane_id == 0, low, pltpu.roll(v, 1, 1))
            after = jnp.where(lane_id == width - 1, high, pltpu.roll(v, width - 1, 1))
            lap_y = (before + after) - 2.0 * v
            react = -8.0 * v * (v - 0.15) * (v - 1.0) - v * w
            drive = into[z * rows : (z + 1) * rows]
            new_v = v + (coef[0, z] * lap_z + coef[1, z] * lap_x + coef[2, z] * lap_y) + 0.1 * (react + drive)
            rec_out[z] = w + 0.01 * (-w - 8.0 * v * (v - 1.15))
            vp[s + 1, z + 1] = new_v
            hx_send[s + 1, 0, z : z + 1, :] = new_v[0:1]
            hx_send[s + 1, 1, z : z + 1, :] = new_v[rows - 1 : rows]
            packed = pack(new_v, z, packed)
        hy_send[s + 1] = packed

        @pl.when(s < STEPS - 1)
        def _():
            send_halos(s + 1)
            v_send[s + 1] = select_dot(a_mat[...], vp[s + 1, 1 : depth + 1].reshape(voxel_rows, width))
            send_slots(v_send, v_recv, s + 1, v_sem_s, v_sem_r)

        all_slots(v_send, v_recv, s, v_sem_s, v_sem_r).wait_recv()
        into_term = select_dot(tgt_mat[...], gain_o[...] * (v_recv[s] - u_send[s]))
        u = tv_out[...]
        r = tr_out[...]
        ends = iota(u.shape, 1)
        before = jnp.where(ends == 0, u, pltpu.roll(u, 1, 1))
        after = jnp.where(ends == width - 1, u, pltpu.roll(u, width - 1, 1))
        lap_k = (before + after) - 2.0 * u
        react = -8.0 * u * (u - 0.15) * (u - 1.0) - u * r
        new_u = u + cable * lap_k + 0.1 * (react + 0.1 * into_term)
        tr_out[...] = r + 0.01 * (-r - 8.0 * u * (u - 1.15))
        tv_out[...] = new_u

        @pl.when(s < STEPS - 1)
        def _():
            u_send[s + 1] = select_dot(tg_mat[...], new_u)
            send_slots(u_send, u_recv, s + 1, u_sem_s, u_sem_r)

        return carry

    lax.fori_loop(0, STEPS, step, 0)
    volt_out[...] = vp[STEPS, 1 : depth + 1]

    all_msgs().wait_send()

    def finish(s, carry):
        for copy, sends, _ in halo_copies(s):
            pl.when(sends)(copy.wait_send)
        all_slots(v_send, v_recv, s, v_sem_s, v_sem_r).wait_send()
        all_slots(u_send, u_recv, s, u_sem_s, u_sem_r).wait_send()
        return carry

    lax.fori_loop(0, STEPS, finish, 0)


def on_device(sizes, volt, recovery, fiber_class, fiber_table, junction_block, junction_term, junction_owner, term_volt, term_recovery, term_gain, cable_gain):
    n_gx, n_gy, n_gz = sizes
    depth, rows, width = volt.shape
    n = n_gx * n_gy
    jcount = junction_block.shape[0]
    terms = term_volt.shape[0]
    most = max(8, 2 * jcount // n)
    cap = 1 << (most - 1).bit_length()
    slots = n * cap
    voxel_rows = depth * rows
    vmem = pl.BlockSpec(memory_space=pltpu.VMEM)
    smem = pl.BlockSpec(memory_space=pltpu.SMEM)
    dma = pltpu.SemaphoreType.DMA
    return pl.pallas_call(
        functools.partial(kernel, n_gx, n_gy, n_gz, cap),
        out_shape=(
            jax.ShapeDtypeStruct(volt.shape, F32),
            jax.ShapeDtypeStruct(volt.shape, F32),
            jax.ShapeDtypeStruct(term_volt.shape, F32),
            jax.ShapeDtypeStruct(term_volt.shape, F32),
        ),
        in_specs=[smem] + [vmem] * 10,
        out_specs=(vmem,) * 4,
        scratch_shapes=[
            pltpu.VMEM((STEPS + 1, depth + 2, rows, width), F32),
            pltpu.VMEM((3, depth, rows, width), F32),
            pltpu.VMEM((voxel_rows, width), F32),
            pltpu.VMEM((slots, voxel_rows), BF16),
            pltpu.VMEM((voxel_rows, slots), BF16),
            pltpu.VMEM((slots, terms), BF16),
            pltpu.VMEM((terms, slots), BF16),
            pltpu.VMEM((slots, width), F32),
            pltpu.VMEM((slots, width), F32),
            pltpu.VMEM((n, 1, 128), F32),
            pltpu.VMEM((n, 1, 128), F32),
            pltpu.VMEM((STEPS, slots, width), F32),
            pltpu.VMEM((STEPS, slots, width), F32),
            pltpu.VMEM((STEPS, slots, width), F32),
            pltpu.VMEM((STEPS, slots, width), F32),
            pltpu.VMEM((STEPS + 1, 2, depth, width), F32),
            pltpu.VMEM((STEPS, 2, depth, width), F32),
            pltpu.VMEM((STEPS + 1, 8, width), F32),
            pltpu.VMEM((STEPS, 2, 8, width), F32),
            dma((2,)),
            dma((STEPS,)),
            dma((STEPS,)),
            dma((STEPS,)),
            dma((STEPS,)),
            dma((STEPS, 6)),
            dma((STEPS, 6)),
        ],
        compiler_params=pltpu.CompilerParams(
            collective_id=0, has_side_effects=True, vmem_limit_bytes=48 * 1024 * 1024
        ),
        name="slab",
    )(
        fiber_table,
        volt,
        recovery,
        fiber_class,
        junction_block.reshape(1, jcount),
        junction_term.reshape(1, jcount),
        junction_owner.reshape(1, jcount),
        term_volt,
        term_recovery,
        term_gain.reshape(1, terms),
        cable_gain.reshape(1, terms),
    )


def solution(mesh):
    sizes = (mesh.shape["gx"], mesh.shape["gy"], mesh.shape["gz"])
    return jax.shard_map(
        functools.partial(on_device, sizes),
        mesh=mesh,
        in_specs=(
            P("gz", "gx", "gy"),
            P("gz", "gx", "gy"),
            P("gz", "gx", "gy"),
            P(),
            P(("gx", "gy", "gz")),
            P(("gx", "gy", "gz")),
            P(("gx", "gy", "gz"), None),
            P(("gx", "gy", "gz"), None),
            P(("gx", "gy", "gz"), None),
            P(("gx", "gy", "gz")),
            P(("gx", "gy", "gz")),
        ),
        out_specs=(
            P("gz", "gx", "gy"),
            P("gz", "gx", "gy"),
            P(("gx", "gy", "gz"), None),
            P(("gx", "gy", "gz"), None),
        ),
        check_vma=False,
    )
```

```python
import functools
import jax
import jax.numpy as jnp
from jax import lax
from jax.experimental import pallas as pl
from jax.experimental.pallas import tpu as pltpu
from jax.sharding import PartitionSpec as P

STEPS = 4
MESH = pl.DeviceIdType.MESH
F32 = jnp.float32
BF16 = jnp.bfloat16
EXACT = lax.Precision.HIGHEST
GAIN_LANE = 64


def iota(shape, dim):
    return lax.broadcasted_iota(jnp.int32, shape, dim)


def one_hot(cond):
    return jnp.where(cond, 1.0, 0.0).astype(BF16)


def dot_nt(a, b):
    return lax.dot_general(a, b, (((1,), (1,)), ((), ())), preferred_element_type=F32)


def select_dot(mask, values):
    high = values.astype(BF16)
    rest = values - high.astype(F32)
    mid = rest.astype(BF16)
    low = (rest - mid.astype(F32)).astype(BF16)
    return (
        jnp.dot(mask, low, preferred_element_type=F32)
        + jnp.dot(mask, mid, preferred_element_type=F32)
    ) + jnp.dot(mask, high, preferred_element_type=F32)


def kernel(
    n_gx,
    n_gy,
    n_gz,
    cap,
    table,
    volt_in,
    rec_in,
    fiber,
    block_row,
    term_row,
    owner_row,
    tv_in,
    tr_in,
    gain_row,
    cable_row,
    volt_out,
    rec_out,
    tv_out,
    tr_out,
    vp,
    coef,
    into,
    klasses,
    same_mat,
    v_base,
    current,
    a_mat,
    at_mat,
    tg_mat,
    tgt_mat,
    gain_h,
    gain_o,
    msg_send,
    msg_recv,
    v_send,
    v_recv,
    u_send,
    u_recv,
    hx_send,
    hx_recv,
    hy_send,
    hy_recv,
    msg_sem,
    v_sem_s,
    v_sem_r,
    u_sem_s,
    u_sem_r,
    halo_s,
    halo_r,
    in_sem,
):
    gx = lax.axis_index("gx")
    gy = lax.axis_index("gy")
    gz = lax.axis_index("gz")
    n = n_gx * n_gy
    me = gx * n_gy + gy
    depth, rows, width = volt_in.shape
    voxel_rows = depth * rows
    groups = voxel_rows // 8
    per = rows // 8
    slots = n * cap
    terms = tv_in.shape[0]
    jcount = block_row.shape[1]
    shift = cap.bit_length() - 1

    def at_peer(d):
        p = lax.rem(me + d, n)
        return p, {"gx": p // n_gy, "gy": lax.rem(p, n_gy)}

    loads = [
        pltpu.make_async_copy(src, dst, in_sem.at[k])
        for k, (src, dst) in enumerate(
            (
                (volt_in, vp.at[0, pl.ds(1, depth)]),
                (fiber, klasses),
                (tv_in, tv_out),
                (tr_in, tr_out),
                (rec_in, rec_out),
            )
        )
    ]

    barrier = pltpu.get_barrier_semaphore()

    def greet(d, carry):
        _, where_to = at_peer(d)
        pl.semaphore_signal(barrier, inc=1, device_id=where_to, device_id_type=MESH)
        return carry

    lax.fori_loop(1, n, greet, 0)

    pl.semaphore_signal(barrier, inc=1, device_id={"gz": n_gz - 1 - gz}, device_id_type=MESH)

    for load in loads:
        load.start()

    def rows_of(p):
        return pl.ds(pl.multiple_of(p * cap, 8), cap)

    def slot_copy(src, dst, s, d, send_sem, recv_sem):
        p, where_to = at_peer(d)
        return pltpu.make_async_remote_copy(
            src_ref=src.at[s, rows_of(p)],
            dst_ref=dst.at[s, rows_of(me)],
            send_sem=send_sem.at[s],
            recv_sem=recv_sem.at[s],
            device_id=where_to,
            device_id_type=MESH,
        )

    def send_slots(src, dst, s, send_sem, recv_sem):
        def go(d, carry):
            slot_copy(src, dst, s, d, send_sem, recv_sem).start()
            return carry

        lax.fori_loop(1, n, go, 0)
        dst[s, rows_of(me)] = src[s, rows_of(me)]

    def all_slots(src, dst, s, send_sem, recv_sem):
        part = pl.ds(0, (n - 1) * cap)
        _, where_to = at_peer(1)
        return pltpu.make_async_remote_copy(
            src_ref=src.at[s, part],
            dst_ref=dst.at[s, part],
            send_sem=send_sem.at[s],
            recv_sem=recv_sem.at[s],
            device_id=where_to,
            device_id_type=MESH,
        )

    def halo_copies(s):
        def make(src, dst, k, where_to):
            return pltpu.make_async_remote_copy(
                src_ref=src,
                dst_ref=dst,
                send_sem=halo_s.at[s, k],
                recv_sem=halo_r.at[s, k],
                device_id=where_to,
                device_id_type=MESH,
            )

        last = depth + 1
        return (
            (make(vp.at[s, depth], vp.at[s, 0], 0, {"gz": n_gz - 1 - gz}), gz == 0, gz == n_gz - 1),
            (make(vp.at[s, 1], vp.at[s, last], 1, {"gz": n_gz - 1 - gz}), gz == n_gz - 1, gz == 0),
            (make(hx_send.at[s, 1], hx_recv.at[s, 0], 2, {"gx": lax.rem(gx + 1, n_gx)}), gx < n_gx - 1, gx > 0),
            (make(hx_send.at[s, 0], hx_recv.at[s, 1], 3, {"gx": lax.rem(gx + n_gx - 1, n_gx)}), gx > 0, gx < n_gx - 1),
            (make(hy_send.at[s], hy_recv.at[s, 0], 4, {"gy": lax.rem(gy + 1, n_gy)}), gy < n_gy - 1, gy > 0),
            (make(hy_send.at[s], hy_recv.at[s, 1], 5, {"gy": lax.rem(gy + n_gy - 1, n_gy)}), gy > 0, gy < n_gy - 1),
        )

    lane8 = iota((8, width), 1)

    def pack(plane, z, packed):
        for i in range(per):
            k = z * per + i
            piece = plane[i * 8 : i * 8 + 8]
            packed = jnp.where(lane8 == k, piece[:, 0:1], packed)
            packed = jnp.where(lane8 == k + groups, piece[:, width - 1 : width], packed)
        return packed

    def send_halos(s):
        for copy, sends, _ in halo_copies(s):
            pl.when(sends)(copy.start)

        @pl.when(gz == 0)
        def _():
            vp[s, 0] = vp[s, 1]

        @pl.when(gz == n_gz - 1)
        def _():
            vp[s, depth + 1] = vp[s, depth]

    owner = jnp.broadcast_to(owner_row[...], (jcount, jcount))
    owner_t = jnp.transpose(owner)
    earlier = (owner_t == owner) & (iota((jcount, jcount), 0) < iota((jcount, jcount), 1))
    rank = jnp.sum(jnp.where(earlier, 1.0, 0.0), axis=0, keepdims=True).astype(jnp.int32)
    slot = owner_row[...] * cap + rank
    holds = iota((slots, jcount), 0) == slot
    holds_b = one_hot(holds)
    tie = one_hot(iota((voxel_rows, jcount), 0) == block_row[...])
    a_mat[...] = dot_nt(holds_b, tie).astype(BF16)
    at_mat[...] = dot_nt(tie, holds_b).astype(BF16)
    term_f = term_row[...].astype(F32) + 1.0
    own_id = jnp.sum(jnp.where(holds, term_f, 0.0), axis=1, keepdims=True)
    slot_lane = iota((slots, 128), 1)
    place = iota((slots, 128), 0) & (cap - 1)
    by_place = jnp.where(slot_lane == place, own_id, 0.0).astype(BF16)
    peer_t = one_hot((iota((n, slots), 1) >> shift) == iota((n, slots), 0))
    ids_out = jnp.dot(peer_t, by_place, preferred_element_type=F32)
    spread = jnp.where(iota((terms, 128), 1) == iota((terms, 128), 0) + GAIN_LANE, 1.0, 0.0)
    gains_lane = jnp.dot(
        jnp.broadcast_to(gain_row[...], (8, terms)), spread, precision=EXACT, preferred_element_type=F32
    )[0:1]
    msg = ids_out + gains_lane
    for p in range(n):
        msg_send[p] = msg[p : p + 1]

    loads[0].wait()
    packed = jnp.zeros((8, width), F32)
    for z in range(depth):
        plane = vp[0, z + 1]
        hx_send[0, 0, z : z + 1, :] = plane[0:1]
        hx_send[0, 1, z : z + 1, :] = plane[rows - 1 : rows]
        packed = pack(plane, z, packed)
    hy_send[0] = packed
    v_send[0] = select_dot(a_mat[...], vp[0, 1 : depth + 1].reshape(voxel_rows, width))

    pl.semaphore_wait(barrier, n)

    def msg_copy(d):
        p, where_to = at_peer(d)
        return pltpu.make_async_remote_copy(
            src_ref=msg_send.at[p],
            dst_ref=msg_recv.at[me],
            send_sem=msg_sem.at[0],
            recv_sem=msg_sem.at[1],
            device_id=where_to,
            device_id_type=MESH,
        )

    def send_msg(d, carry):
        msg_copy(d).start()
        return carry

    lax.fori_loop(1, n, send_msg, 0)
    msg_recv[me] = msg_send[me]
    send_halos(0)
    send_slots(v_send, v_recv, 0, v_sem_s, v_sem_r)

    loads[1].wait()
    for z in range(depth):
        klass = klasses[z]
        for k in range(3):
            value = jnp.full(klass.shape, table[k, 0], F32)
            for c in range(1, table.shape[1]):
                value = jnp.where(klass == c, table[k, c], value)
            coef[k, z] = value

    cable = jnp.sum(
        jnp.where(iota((terms, terms), 0) == iota((terms, terms), 1), cable_row[...], 0.0),
        axis=1,
        keepdims=True,
    )

    def all_msgs():
        _, where_to = at_peer(1)
        part = pl.ds(0, n - 1)
        return pltpu.make_async_remote_copy(
            src_ref=msg_send.at[part],
            dst_ref=msg_recv.at[part],
            send_sem=msg_sem.at[0],
            recv_sem=msg_sem.at[1],
            device_id=where_to,
            device_id_type=MESH,
        )

    all_msgs().wait_recv()
    arrived = msg_recv[...].reshape(n, 128)
    peer = jnp.where((iota((slots, n), 0) >> shift) == iota((slots, n), 1), 1.0, 0.0)
    per_slot = jnp.dot(peer, arrived, precision=EXACT, preferred_element_type=F32)
    far_id = jnp.sum(jnp.where(slot_lane == place, per_slot, 0.0), axis=1, keepdims=True)
    far_id = (far_id + 0.5).astype(jnp.int32) - 1
    own_at = (own_id + 0.5).astype(jnp.int32) - 1
    gain_own = jnp.sum(
        jnp.where((slot_lane == own_at + GAIN_LANE) & (own_at >= 0), per_slot, 0.0), axis=1, keepdims=True
    )
    gain_far = jnp.sum(
        jnp.where((slot_lane == far_id + GAIN_LANE) & (far_id >= 0), gains_lane, 0.0), axis=1, keepdims=True
    )
    gain_h[...] = jnp.broadcast_to(gain_own, (slots, width))
    gain_o[...] = jnp.broadcast_to(gain_far, (slots, width))
    tg = one_hot(iota((slots, terms), 1) == far_id)
    tg_mat[...] = tg
    tgt_mat[...] = dot_nt(one_hot(iota((terms, terms), 0) == iota((terms, terms), 1)), tg).astype(BF16)

    loads[2].wait()
    u_send[0] = select_dot(tg, tv_out[...])
    send_slots(u_send, u_recv, 0, u_sem_s, u_sem_r)

    same_mat[...] = dot_nt(a_mat[...], a_mat[...]).astype(BF16)
    loads[3].wait()
    loads[4].wait()
    row_id = iota((rows, width), 0)
    lane_id = iota((rows, width), 1)

    def base(s):
        for copy, _, receives in halo_copies(s):
            pl.when(receives)(copy.wait_recv)
        mirrored = pltpu.roll(hy_send[s], groups, 1)
        left = jnp.where(gy == 0, mirrored, hy_recv[s, 0])
        right = jnp.where(gy == n_gy - 1, mirrored, hy_recv[s, 1])
        for z in range(depth):
            v = vp[s, z + 1]
            w = rec_out[z]
            lap_z = (vp[s, z + 2] + vp[s, z]) - 2.0 * v
            above = jnp.where(gx == n_gx - 1, v[rows - 1 : rows], hx_recv[s, 1, z : z + 1, :])
            below = jnp.where(gx == 0, v[0:1], hx_recv[s, 0, z : z + 1, :])
            up = jnp.where(row_id == rows - 1, above, pltpu.roll(v, rows - 1, 0))
            down = jnp.where(row_id == 0, below, pltpu.roll(v, 1, 0))
            lap_x = (up + down) - 2.0 * v
            k = z * per
            low = jnp.concatenate([left[:, groups + k + i : groups + k + i + 1] for i in range(per)], axis=0)
            high = jnp.concatenate([right[:, k + i : k + i + 1] for i in range(per)], axis=0)
            before = jnp.where(lane_id == 0, low, pltpu.roll(v, 1, 1))
            after = jnp.where(lane_id == width - 1, high, pltpu.roll(v, width - 1, 1))
            lap_y = (before + after) - 2.0 * v
            react = -8.0 * v * (v - 0.15) * (v - 1.0) - v * w
            vp[s + 1, z + 1] = v + (coef[0, z] * lap_z + coef[1, z] * lap_x + coef[2, z] * lap_y) + 0.1 * react
            rec_out[z] = w + 0.01 * (-w - 8.0 * v * (v - 1.15))

        @pl.when(s < STEPS - 1)
        def _():
            v_base[...] = select_dot(a_mat[...], vp[s + 1, 1 : depth + 1].reshape(voxel_rows, width))

    def currents(s):
        all_slots(u_send, u_recv, s, u_sem_s, u_sem_r).wait_recv()
        current[...] = gain_h[...] * (u_recv[s] - v_send[s])

        @pl.when(s < STEPS - 1)
        def _():
            v_send[s + 1] = v_base[...] + 0.1 * select_dot(same_mat[...], current[...])
            send_slots(v_send, v_recv, s + 1, v_sem_s, v_sem_r)

    def voxels(s):
        into[...] = select_dot(at_mat[...], current[...])
        packed = jnp.zeros((8, width), F32)
        for z in range(depth):
            new_v = vp[s + 1, z + 1] + 0.1 * into[z * rows : (z + 1) * rows]
            vp[s + 1, z + 1] = new_v
            hx_send[s + 1, 0, z : z + 1, :] = new_v[0:1]
            hx_send[s + 1, 1, z : z + 1, :] = new_v[rows - 1 : rows]
            packed = pack(new_v, z, packed)
        hy_send[s + 1] = packed

        @pl.when(s < STEPS - 1)
        def _():
            send_halos(s + 1)

    def terminals(s):
        all_slots(v_send, v_recv, s, v_sem_s, v_sem_r).wait_recv()
        into_term = select_dot(tgt_mat[...], gain_o[...] * (v_recv[s] - u_send[s]))
        u = tv_out[...]
        r = tr_out[...]
        ends = iota(u.shape, 1)
        before = jnp.where(ends == 0, u, pltpu.roll(u, 1, 1))
        after = jnp.where(ends == width - 1, u, pltpu.roll(u, width - 1, 1))
        lap_k = (before + after) - 2.0 * u
        react = -8.0 * u * (u - 0.15) * (u - 1.0) - u * r
        new_u = u + cable * lap_k + 0.1 * (react + 0.1 * into_term)
        tr_out[...] = r + 0.01 * (-r - 8.0 * u * (u - 1.15))
        tv_out[...] = new_u

        @pl.when(s < STEPS - 1)
        def _():
            u_send[s + 1] = select_dot(tg_mat[...], new_u)
            send_slots(u_send, u_recv, s + 1, u_sem_s, u_sem_r)

    def two_steps(i, carry):
        s = 2 * i
        base(s)
        terminals(s)
        currents(s)
        voxels(s)
        base(s + 1)
        currents(s + 1)
        voxels(s + 1)
        terminals(s + 1)
        return carry

    lax.fori_loop(0, STEPS // 2, two_steps, 0)
    volt_out[...] = vp[STEPS, 1 : depth + 1]

    all_msgs().wait_send()

    def finish(s, carry):
        for copy, sends, _ in halo_copies(s):
            pl.when(sends)(copy.wait_send)
        all_slots(v_send, v_recv, s, v_sem_s, v_sem_r).wait_send()
        all_slots(u_send, u_recv, s, u_sem_s, u_sem_r).wait_send()
        return carry

    lax.fori_loop(0, STEPS, finish, 0)


def on_device(sizes, volt, recovery, fiber_class, fiber_table, junction_block, junction_term, junction_owner, term_volt, term_recovery, term_gain, cable_gain):
    n_gx, n_gy, n_gz = sizes
    depth, rows, width = volt.shape
    n = n_gx * n_gy
    jcount = junction_block.shape[0]
    terms = term_volt.shape[0]
    most = max(8, 2 * jcount // n)
    cap = 1 << (most - 1).bit_length()
    slots = n * cap
    voxel_rows = depth * rows
    vmem = pl.BlockSpec(memory_space=pltpu.VMEM)
    hbm = pl.BlockSpec(memory_space=pltpu.HBM)
    smem = pl.BlockSpec(memory_space=pltpu.SMEM)
    dma = pltpu.SemaphoreType.DMA
    return pl.pallas_call(
        functools.partial(kernel, n_gx, n_gy, n_gz, cap),
        out_shape=(
            jax.ShapeDtypeStruct(volt.shape, F32),
            jax.ShapeDtypeStruct(volt.shape, F32),
            jax.ShapeDtypeStruct(term_volt.shape, F32),
            jax.ShapeDtypeStruct(term_volt.shape, F32),
        ),
        in_specs=[smem] + [hbm] * 3 + [vmem] * 3 + [hbm] * 2 + [vmem] * 2,
        out_specs=(vmem,) * 4,
        scratch_shapes=[
            pltpu.VMEM((STEPS + 1, depth + 2, rows, width), F32),
            pltpu.VMEM((3, depth, rows, width), F32),
            pltpu.VMEM((voxel_rows, width), F32),
            pltpu.VMEM((depth, rows, width), jnp.int32),
            pltpu.VMEM((slots, slots), BF16),
            pltpu.VMEM((slots, width), F32),
            pltpu.VMEM((slots, width), F32),
            pltpu.VMEM((slots, voxel_rows), BF16),
            pltpu.VMEM((voxel_rows, slots), BF16),
            pltpu.VMEM((slots, terms), BF16),
            pltpu.VMEM((terms, slots), BF16),
            pltpu.VMEM((slots, width), F32),
            pltpu.VMEM((slots, width), F32),
            pltpu.VMEM((n, 1, 128), F32),
            pltpu.VMEM((n, 1, 128), F32),
            pltpu.VMEM((STEPS, slots, width), F32),
            pltpu.VMEM((STEPS, slots, width), F32),
            pltpu.VMEM((STEPS, slots, width), F32),
            pltpu.VMEM((STEPS, slots, width), F32),
            pltpu.VMEM((STEPS + 1, 2, depth, width), F32),
            pltpu.VMEM((STEPS, 2, depth, width), F32),
            pltpu.VMEM((STEPS + 1, 8, width), F32),
            pltpu.VMEM((STEPS, 2, 8, width), F32),
            dma((2,)),
            dma((STEPS,)),
            dma((STEPS,)),
            dma((STEPS,)),
            dma((STEPS,)),
            dma((STEPS, 6)),
            dma((STEPS, 6)),
            dma((5,)),
        ],
        compiler_params=pltpu.CompilerParams(
            collective_id=0, has_side_effects=True, vmem_limit_bytes=64 * 1024 * 1024 - 65536
        ),
        name="slab",
    )(
        fiber_table,
        volt,
        recovery,
        fiber_class,
        junction_block.reshape(1, jcount),
        junction_term.reshape(1, jcount),
        junction_owner.reshape(1, jcount),
        term_volt,
        term_recovery,
        term_gain.reshape(1, terms),
        cable_gain.reshape(1, terms),
    )


def solution(mesh):
    sizes = (mesh.shape["gx"], mesh.shape["gy"], mesh.shape["gz"])
    return jax.shard_map(
        functools.partial(on_device, sizes),
        mesh=mesh,
        in_specs=(
            P("gz", "gx", "gy"),
            P("gz", "gx", "gy"),
            P("gz", "gx", "gy"),
            P(),
            P(("gx", "gy", "gz")),
            P(("gx", "gy", "gz")),
            P(("gx", "gy", "gz"), None),
            P(("gx", "gy", "gz"), None),
            P(("gx", "gy", "gz"), None),
            P(("gx", "gy", "gz")),
            P(("gx", "gy", "gz")),
        ),
        out_specs=(
            P("gz", "gx", "gy"),
            P("gz", "gx", "gy"),
            P(("gx", "gy", "gz"), None),
            P(("gx", "gy", "gz"), None),
        ),
        check_vma=False,
    )
```
